32 devices in a mesh: ma: 8 (over y, x, core), row: 4 (over z).
Axes of the slice: x: 2, y: 2, z: 4, core: 2. Of those that a mesh axis runs over, the one named last changes fastest.
Arguments:
- velocity: bfloat16 [3, 2, 384, 128, 384], P(None, None, 'ma', 'row'), may hold values from -6 to 6
- vorticity: bfloat16 [3, 2, 384, 128, 384], P(None, None, 'ma', 'row'), may hold values from -6 to 6
- order_table: int32 [384], replicated, may hold values from 0 to 383, as said below
- legendre_bf: bfloat16 [384, 384, 576], P('ma'), may hold values from -24 to 24, as said below
- weighted: bfloat16 [384, 384, 576], P('ma'), may hold values from -1 to 1, as said below
- inverse_operators: float32 [384, 128, 128], P('row'), may hold values from -1.5 to 1.5
Outputs:
- advanced: float32 [3, 2, 384, 384, 128], P(None, None, 'ma', 'row')
The draws below stay inside these ranges and needn't reach their ends.
Inputs may be any that keep to these rules, and one draw needn't show every extreme that they name: `order_table`: slots 2k and 2k + 1 hold wavenumbers that add up to 383, and every wavenumber from 0 to 383 stands in exactly one slot. legendre_bf[slot, l, j] is Pbar_l^m(x_j) rounded to bfloat16, with m = order_table[slot], x_j = cos(pi (j + 0.5) / 576), s_j = sin(pi (j + 0.5) / 576), zero for l < m, Pbar_m^m = exp(-0.5 log 2 + 0.5 (lgamma(m + 1.5) - lgamma(m + 1) - lgamma(1.5)) + m log s_j) and Pbar_l^m = a (x_j Pbar_(l-1)^m - b Pbar_(l-2)^m), a = sqrt((4 l^2 - 1) / (l^2 - m^2)), b = sqrt(((l - 1)^2 - m^2) / (4 (l - 1)^2 - 1)). weighted[slot, l, j] is w_j Pbar_l^m(x_j), computed in float32 and rounded to bfloat16, with w_j = pi s_j / 576.
All inputs are finite; a program needn't handle non-finite values.
Results may differ from the reference program's by a relative error of at most 0.005.
Values may be sent and summed in bfloat16 or wider, within the bound.
A program may use at most 256 MiB of HBM per device.

```python
import math
import jax
import jax.numpy as jnp
from jax import lax

NL = 384
NLAT = 576
NLON = 1152
NR = 128
NM = 384
N_MA = 8


rescale_limit = 10000000000.0


rescale_log = 23.025850929940457


gamma_offset = 0.06039111881762261


def order_pairs(key):
    pair_low = jax.random.permutation(jax.random.fold_in(key, 11), NL // 2).astype(jnp.int32)
    return jnp.stack([pair_low, NL - 1 - pair_low], axis=1).reshape(NL).astype(jnp.int32)


def legendre_values(key):
    orders = order_pairs(key)
    angles = (jnp.arange(NLAT, dtype=jnp.float32) + 0.5) * (math.pi / NLAT)
    cosines = jnp.cos(angles)
    sine_values = jnp.sin(angles)
    order_value = orders.astype(jnp.float32)[:, None]
    order_index = orders.astype(jnp.int32)[:, None]
    order_square = order_value * order_value
    log_start = -0.5 * math.log(2.0) + gamma_offset + 0.5 * (lax.lgamma(order_value + 1.5) - lax.lgamma(order_value + 1.0)) + order_value * jnp.log(sine_values)[None, :]
    cosine_row = cosines[None, :]
    start_zero = jnp.zeros(log_start.shape, jnp.float32)
    start_one = jnp.ones(log_start.shape, jnp.float32)

    def advance(carried, degree):
        earlier, current, log_scale = carried
        degree_value = degree.astype(jnp.float32)
        lower_degree = degree_value - 1.0
        moving = degree > order_index
        factor_up = jnp.sqrt(jnp.maximum(4.0 * degree_value * degree_value - 1.0, 1.0) / jnp.maximum(degree_value * degree_value - order_square, 1.0))
        factor_back = jnp.sqrt(jnp.maximum(lower_degree * lower_degree - order_square, 0.0) / jnp.maximum(4.0 * lower_degree * lower_degree - 1.0, 1.0))
        updated = factor_up * (cosine_row * current - factor_back * earlier)
        following = jnp.where(moving, updated, current)
        previous = jnp.where(moving, current, earlier)
        too_large = jnp.abs(following) > rescale_limit
        following = jnp.where(too_large, following / rescale_limit, following)
        previous = jnp.where(too_large, previous / rescale_limit, previous)
        log_scale = jnp.where(too_large, log_scale + rescale_log, log_scale)
        emitted = jnp.where(degree >= order_index, following * jnp.exp(log_scale), 0.0)
        return ((previous, following, log_scale), emitted)
    degree_list = jnp.arange(NL, dtype=jnp.int32)
    final_state, values = lax.scan(advance, (start_zero, start_one, log_start), degree_list)
    return (jnp.transpose(values, (1, 0, 2)), sine_values)


def draw_order_table(key, part):
    return order_pairs(key)


def draw_legendre_bf(key, part):
    values, sine_values = legendre_values(key)
    return values.astype(jnp.bfloat16)


def draw_weighted(key, part):
    values, sine_values = legendre_values(key)
    quad_weights = sine_values * (math.pi / NLAT)
    return (values * quad_weights[None, None, :]).astype(jnp.bfloat16)


def draw_inverse_operators(key, part):
    key_diag = jax.random.fold_in(key, 21)
    key_coupling = jax.random.fold_in(key, 22)
    diagonal = jax.random.uniform(key_diag, (NL, NR), jnp.float32, 0.5, 1.0)
    coupling = jax.random.normal(key_coupling, (NL, NR, NR), jnp.float32)
    identity = jnp.eye(NR, dtype=jnp.float32)
    return coupling * (0.6 / math.sqrt(NR)) + identity[None, :, :] * diagonal[:, :, None]


def block_levels(rng, extent, cuts, smallest, top_value):
    level, own = 1.0, jax.random.fold_in(rng, 6)
    for dim, parts in cuts:
        draws = jnp.exp(jax.random.uniform(jax.random.fold_in(own, dim), (parts,), jnp.float32, smallest / len(cuts), top_value / len(cuts)))
        level = level * jnp.repeat(draws, extent[dim] // parts).reshape([-1 if axis == dim else 1 for axis in range(len(extent))])
    return level


def scatter_about(key, shape, scale, reach, cuts=(), kind=jnp.bfloat16):
    drawn = scale * jax.random.normal(key, shape, jnp.float32)
    if cuts:
        drawn = drawn * block_levels(key, shape, cuts, -0.22, 0.18)
    return jnp.clip(drawn, -reach, reach).astype(kind)


def setup_inputs(seed: int = 0) -> dict:
    keys = jax.random.split(jax.random.key(seed), 7)
    return {
        "velocity": scatter_about(keys[0], (3, 2, NM, NR, NL), 1.0, 6.0, ((2, 8), (3, 4))),
        "vorticity": scatter_about(keys[1], (3, 2, NM, NR, NL), 1.0, 6.0, ((2, 8), (3, 4))),
        "order_table": draw_order_table(jax.random.fold_in(keys[6], 71), 0),
        "legendre_bf": draw_legendre_bf(jax.random.fold_in(keys[6], 71), 0),
        "weighted": draw_weighted(jax.random.fold_in(keys[6], 71), 0),
        "inverse_operators": draw_inverse_operators(jax.random.fold_in(keys[6], 71), 0),
    }


time_step = 0.5
rotation = 2.0


def longitude_table(orders):
    points = jnp.arange(NLON, dtype=jnp.int32)
    phases = (orders.astype(jnp.int32)[:, None] * points[None, :]) % NLON
    angles = phases.astype(jnp.float32) * (2.0 * math.pi / NLON)
    return jnp.stack([jnp.cos(angles), -jnp.sin(angles)]).astype(jnp.bfloat16)


def cross_terms(moving, spinning):
    spin_total = spinning[2] + rotation
    component_one = moving[1] * spin_total - moving[2] * spinning[1]
    component_two = moving[2] * spinning[0] - moving[0] * spin_total
    component_three = moving[0] * spinning[1] - moving[1] * spinning[0]
    return jnp.stack([component_one, component_two, component_three])


def reference(velocity, vorticity, order_table, legendre_bf, weighted, inverse_operators):
    highest = lax.Precision.HIGHEST
    slot_block = NM // N_MA
    lat_block = NLAT // N_MA
    spectral = jnp.concatenate([velocity, vorticity], axis=0)
    spec_blocks = spectral.reshape(6, 2, N_MA, slot_block, NR, NL).transpose(2, 0, 1, 3, 4, 5)
    table_blocks = legendre_bf.reshape(N_MA, slot_block, NL, NLAT)
    weight_blocks = weighted.reshape(N_MA, slot_block, NL, NLAT)
    slot_scale = jnp.where(order_table == 0, 1.0, 2.0).astype(jnp.float32) / NL
    scale_blocks = slot_scale.reshape(N_MA, slot_block)

    def synthesize(pieces):
        block_spec, block_table, block_scale = pieces
        grid_values = jnp.einsum('cpsrl,slt->cpsrt', block_spec.astype(jnp.float32),
                                 block_table.astype(jnp.float32), precision=highest)
        return (grid_values * block_scale[None, None, :, None, None]).astype(jnp.bfloat16)

    grid_blocks = lax.map(synthesize, (spec_blocks, table_blocks, scale_blocks))
    grid_spec = grid_blocks.transpose(1, 2, 0, 3, 4, 5).reshape(6, 2, NM, NR, NLAT)
    harmonics = longitude_table(order_table).astype(jnp.float32)
    lat_pieces = grid_spec.reshape(6, 2, NM, NR, N_MA, lat_block).transpose(4, 0, 1, 2, 3, 5)

    def nonlinear(lat_piece):
        grid_values = jnp.einsum('cpsrt,psn->crtn', lat_piece.astype(jnp.float32),
                                 harmonics, precision=highest)
        products = cross_terms(grid_values[:3], grid_values[3:]).astype(jnp.bfloat16)
        spectral_back = jnp.einsum('crtn,psn->cpsrt', products.astype(jnp.float32),
                                   harmonics, precision=highest)
        return ((NL / NLON) * spectral_back).astype(jnp.bfloat16)

    gathered_terms = lax.map(nonlinear, lat_pieces)
    tendency_grid = gathered_terms.transpose(1, 2, 3, 4, 0, 5).reshape(3, 2, NM, NR, NLAT)
    tend_blocks = tendency_grid.reshape(3, 2, N_MA, slot_block, NR, NLAT).transpose(2, 0, 1, 3, 4, 5)

    def analyze(pieces):
        block_terms, block_weights = pieces
        return jnp.einsum('cpsrt,slt->cpsrl', block_terms.astype(jnp.float32),
                          block_weights.astype(jnp.float32), precision=highest)

    term_blocks = lax.map(analyze, (tend_blocks, weight_blocks))
    spec_terms = term_blocks.transpose(1, 2, 0, 3, 4, 5).reshape(3, 2, NM, NR, NL)
    right_side = velocity.astype(jnp.float32) + time_step * spec_terms
    return jnp.einsum('lab,cpsbl->cpsla', inverse_operators, right_side, precision=highest)
```

```python
import functools
import math

import jax
import jax.numpy as jnp
from jax import lax
from jax.experimental import pallas as pl
from jax.experimental.pallas import tpu as pltpu
from jax.sharding import PartitionSpec as P

NL = 384
NLAT = 576
NLON = 1152
NR = 128


LANES = 128
ROWS = 16


time_step = 0.5
rotation = 2.0


def longitude_table(orders):
    points = jnp.arange(NLON, dtype=jnp.int32)
    phases = orders[:, None] * points[None, :] % NLON
    angles = phases.astype(jnp.float32) * (2.0 * math.pi / NLON)
    return jnp.stack([jnp.cos(angles), -jnp.sin(angles)]).astype(jnp.bfloat16)


def cross_terms(moving, spinning):
    spin_total = spinning[2] + rotation
    component_one = moving[1] * spin_total - moving[2] * spinning[1]
    component_two = moving[2] * spinning[0] - moving[0] * spin_total
    component_three = moving[0] * spinning[1] - moving[1] * spinning[0]
    return component_one, component_two, component_three


def synth_kernel(scale_ref, spec_ref, table_ref, early_ref, late_ref, turned):
    comps, parts, slots, radii, degrees = spec_ref.shape
    lat = table_ref.shape[2]
    half = radii // 2
    rows = comps * parts * half
    first_slot = pl.program_id(0) * slots
    for s in range(slots):
        spec = spec_ref[:, :, s].reshape(2 * rows, degrees)
        sums = jnp.dot(spec, table_ref[s], preferred_element_type=jnp.float32)
        sums = (sums * scale_ref[first_slot + s]).reshape(comps * parts, 2, half, lat)
        wide = jnp.concatenate(
            [sums[:, 0].reshape(rows, lat), sums[:, 1].reshape(rows, lat)], axis=1
        )
        for t in range(2 * lat // LANES):
            turned[t, pl.ds(s, rows, stride=slots), :] = wide[:, t * LANES : (t + 1) * LANES]
    owners = half // 2
    for i in range(comps * parts):
        c, p = i // parts, i % parts
        for h, out_ref in enumerate((early_ref, late_ref)):
            for d in range(owners):
                row = (i * half + h * owners + d) * slots
                for t in range(2 * lat // LANES):
                    out_ref[d, c, p, :, t * LANES : (t + 1) * LANES] = turned[
                        t, pl.ds(row, slots), :
                    ].astype(jnp.bfloat16)


def synthesize(spec, table, scale):
    comps, parts, slots, radii, degrees = spec.shape
    lat = table.shape[2]
    owners = radii // 4
    shape = jax.ShapeDtypeStruct((owners, comps, parts, slots, 2 * lat), jnp.bfloat16)
    out_spec = pl.BlockSpec((owners, comps, parts, ROWS, 2 * lat), lambda i: (0, 0, 0, i, 0))
    rows = comps * parts * radii // 2 * ROWS
    return pl.pallas_call(
        synth_kernel,
        grid=(slots // ROWS,),
        in_specs=[
            pl.BlockSpec(memory_space=pltpu.SMEM),
            pl.BlockSpec((comps, parts, ROWS, radii, degrees), lambda i: (0, 0, i, 0, 0)),
            pl.BlockSpec((ROWS, degrees, lat), lambda i: (i, 0, 0)),
        ],
        out_specs=[out_spec, out_spec],
        out_shape=[shape, shape],
        scratch_shapes=[pltpu.VMEM((2 * lat // LANES, rows, LANES), jnp.float32)],
        compiler_params=pltpu.CompilerParams(vmem_limit_bytes=56 << 20),
        cost_estimate=pl.CostEstimate(
            flops=2 * spec.size * lat,
            bytes_accessed=2 * (spec.size + table.size + spec.size * lat // degrees),
            transcendentals=0,
        ),
    )(scale, spec, table)


def grid_kernel(scale, move_ref, spin_ref, across_ref, along_ref, out_ref, packed, total):
    owners, comps, parts, slots, wide = move_ref.shape
    waves = owners * parts * slots
    points = along_ref.shape[1]
    for c in range(comps):
        packed[:, c * wide : (c + 1) * wide] = move_ref[:, c].reshape(waves, wide)
        packed[:, (comps + c) * wide : (comps + c + 1) * wide] = spin_ref[:, c].reshape(waves, wide)
    step = points // 3
    for k in range(3):
        grid = jnp.dot(
            across_ref[k * step : (k + 1) * step, :],
            packed[...],
            preferred_element_type=jnp.float32,
        )
        fields = [grid[:, i * wide : (i + 1) * wide] for i in range(2 * comps)]
        products = jnp.concatenate(cross_terms(fields[:3], fields[3:]), axis=1)
        part = jnp.dot(
            along_ref[:, k * step : (k + 1) * step],
            products.astype(jnp.bfloat16),
            preferred_element_type=jnp.float32,
        )
        total[...] = part if k == 0 else total[...] + part
    for c in range(comps):
        back = (scale * total[:, c * wide : (c + 1) * wide]).astype(jnp.bfloat16)
        out_ref[:, c] = back.reshape(owners, parts, slots, wide)


def through_grid(moving, spinning, across, along, scale):
    owners, comps, parts, slots, columns = moving.shape
    waves, points = along.shape
    wide = columns // 3
    block = pl.BlockSpec((owners, comps, parts, slots, wide), lambda i: (0, 0, 0, 0, i))
    return pl.pallas_call(
        functools.partial(grid_kernel, scale),
        grid=(columns // wide,),
        in_specs=[
            block,
            block,
            pl.BlockSpec((points, waves), lambda i: (0, 0)),
            pl.BlockSpec((waves, points), lambda i: (0, 0)),
        ],
        out_specs=block,
        out_shape=jax.ShapeDtypeStruct(moving.shape, jnp.bfloat16),
        scratch_shapes=[
            pltpu.VMEM((waves, 2 * comps * wide), jnp.bfloat16),
            pltpu.VMEM((waves, comps * wide), jnp.float32),
        ],
        compiler_params=pltpu.CompilerParams(vmem_limit_bytes=56 << 20),
        cost_estimate=pl.CostEstimate(
            flops=2 * 3 * comps * waves * points * columns,
            bytes_accessed=6 * moving.size,
            transcendentals=0,
        ),
    )(moving, spinning, across, along)


def analyze_kernel(early_ref, late_ref, table_ref, velocity_ref, out_ref, turned):
    comps, parts, slots, radii, degrees = velocity_ref.shape
    lat = table_ref.shape[2]
    half = radii // 2
    rows = comps * parts * half
    owners = half // 2
    for i in range(comps * parts):
        c, p = i // parts, i % parts
        for h, in_ref in enumerate((early_ref, late_ref)):
            for d in range(owners):
                row = (i * half + h * owners + d) * slots
                for t in range(2 * lat // LANES):
                    turned[t, pl.ds(row, slots), :] = in_ref[
                        d, c, p, :, t * LANES : (t + 1) * LANES
                    ].astype(jnp.float32)
    for s in range(slots):
        wide = jnp.concatenate(
            [
                turned[t, pl.ds(s, rows, stride=slots), :]
                for t in range(2 * lat // LANES)
            ],
            axis=1,
        )
        pieces = [wide[:, :lat], wide[:, lat:]]
        pieces = [x.astype(jnp.bfloat16).reshape(comps * parts, 1, half, lat) for x in pieces]
        left = jnp.concatenate(pieces, axis=1).reshape(2 * rows, lat)
        terms = lax.dot_general(
            left, table_ref[s], (((1,), (1,)), ((), ())), preferred_element_type=jnp.float32
        )
        terms = terms.reshape(comps, parts, radii, degrees)
        sides = velocity_ref[:, :, s].astype(jnp.float32) + time_step * terms
        out_ref[:, :, s] = sides.astype(jnp.bfloat16)


def analyze(early, late, table, velocity):
    comps, parts, slots, radii, degrees = velocity.shape
    lat = table.shape[2]
    owners = radii // 4
    block = pl.BlockSpec((owners, comps, parts, ROWS, 2 * lat), lambda i: (0, 0, 0, i, 0))
    spec_block = pl.BlockSpec((comps, parts, ROWS, radii, degrees), lambda i: (0, 0, i, 0, 0))
    rows = comps * parts * radii // 2 * ROWS
    return pl.pallas_call(
        analyze_kernel,
        grid=(slots // ROWS,),
        in_specs=[
            block,
            block,
            pl.BlockSpec((ROWS, degrees, lat), lambda i: (i, 0, 0)),
            spec_block,
        ],
        out_specs=spec_block,
        out_shape=jax.ShapeDtypeStruct(velocity.shape, jnp.bfloat16),
        scratch_shapes=[pltpu.VMEM((2 * lat // LANES, rows, LANES), jnp.float32)],
        compiler_params=pltpu.CompilerParams(vmem_limit_bytes=56 << 20),
        cost_estimate=pl.CostEstimate(
            flops=2 * velocity.size * lat,
            bytes_accessed=2 * (3 * velocity.size + table.size),
            transcendentals=0,
        ),
    )(early, late, table, velocity)


def radial_solve(right_side, inverse_operators):
    comps, parts, slots, radii, degrees = right_side.shape
    own, full = inverse_operators.shape[:2]
    groups = full // radii
    split = right_side.reshape(comps, parts, slots, radii, groups, own)
    split = jnp.transpose(split, (4, 5, 0, 1, 2, 3))
    split = split.reshape(groups, own, comps * parts * slots * radii)
    pieces = lax.all_to_all(split, "row", split_axis=0, concat_axis=0, tiled=True)
    columns = pieces.reshape(groups, own, comps, parts, slots, radii)
    operators = inverse_operators.astype(jnp.bfloat16).reshape(own, full, groups, radii)
    return jnp.einsum(
        "qlcpsr,laqr->cpsla", columns, operators, preferred_element_type=jnp.float32
    )


def fits(velocity, legendre_bf, owners):
    return (
        velocity.shape[3] == 4 * owners
        and velocity.shape[3] % (2 * ROWS) == 0
        and velocity.shape[2] % ROWS == 0
        and (2 * legendre_bf.shape[2]) % (3 * LANES) == 0
    )


def by_radius(velocity, vorticity, order_table, legendre_bf, weighted, inverse_operators):
    owners = lax.axis_size("ma")
    slots = velocity.shape[2]
    own_orders = lax.dynamic_slice_in_dim(order_table, lax.axis_index("ma") * slots, slots)
    scale = jnp.where(own_orders == 0, 1.0, 2.0).astype(jnp.float32) / NL

    def exchange(x):
        return lax.all_to_all(x, "ma", split_axis=0, concat_axis=0, tiled=True)

    move_early, move_late = synthesize(velocity, legendre_bf, scale)
    spin_early, spin_late = synthesize(vorticity, legendre_bf, scale)
    move_early, spin_early = exchange(move_early), exchange(spin_early)
    move_late, spin_late = exchange(move_late), exchange(spin_late)
    table = longitude_table(order_table).reshape(2, owners, slots, NLON)
    along = jnp.transpose(table, (1, 0, 2, 3)).reshape(2 * owners * slots, NLON)
    across = jnp.transpose(along)
    early = exchange(through_grid(move_early, spin_early, across, along, NL / NLON))
    late = exchange(through_grid(move_late, spin_late, across, along, NL / NLON))
    right_side = analyze(early, late, weighted, velocity)
    return radial_solve(right_side, inverse_operators)


def per_device(velocity, vorticity, order_table, legendre_bf, weighted, inverse_operators):
    if fits(velocity, legendre_bf, lax.axis_size("ma")):
        return by_radius(
            velocity, vorticity, order_table, legendre_bf, weighted, inverse_operators
        )
    slot_count = velocity.shape[2]
    radius_count = velocity.shape[3]
    degree_count = inverse_operators.shape[0]
    own_orders = lax.dynamic_slice_in_dim(
        order_table, lax.axis_index("ma") * slot_count, slot_count
    )
    own_scale = jnp.where(own_orders == 0, 1.0, 2.0).astype(jnp.float32) / NL
    harmonics = longitude_table(order_table)

    def arrange(grid_values):
        scaled = (grid_values * own_scale[None, None, :, None, None]).astype(jnp.bfloat16)
        ordered = jnp.transpose(scaled, (0, 1, 2, 4, 3))
        return ordered.reshape(3, 2, slot_count, NLAT * radius_count)

    def synthesize(spectral):
        grid_values = jnp.einsum(
            "cpsrl,slt->cpsrt", spectral, legendre_bf, preferred_element_type=jnp.float32
        )
        return arrange(grid_values)

    def to_longitude(pieces):
        return jnp.einsum("cpsk,psn->ckn", pieces, harmonics, preferred_element_type=jnp.float32)

    velocity_grid = to_longitude(
        lax.all_to_all(synthesize(velocity), "ma", split_axis=3, concat_axis=2, tiled=True)
    )
    vorticity_grid = to_longitude(
        lax.all_to_all(synthesize(vorticity), "ma", split_axis=3, concat_axis=2, tiled=True)
    )
    products = jnp.stack(cross_terms(velocity_grid, vorticity_grid)).astype(jnp.bfloat16)
    spectral_back = jnp.einsum(
        "ckn,psn->cpsk", products, harmonics, preferred_element_type=jnp.float32
    )
    spectral_back = (NL / NLON * spectral_back).astype(jnp.bfloat16)
    pieces = lax.all_to_all(spectral_back, "ma", split_axis=2, concat_axis=3, tiled=True)
    field_count = pieces.shape[0]
    split_pieces = pieces.reshape(field_count, 2, slot_count, NLAT, radius_count)
    terms = jnp.einsum(
        "cpstr,slt->cpslr", split_pieces, weighted, preferred_element_type=jnp.float32
    )
    spec_terms = terms.reshape(field_count, 2, slot_count, NL * radius_count)
    velocity_terms = jnp.transpose(velocity.astype(jnp.float32), (0, 1, 2, 4, 3)).reshape(
        3, 2, slot_count, NL * radius_count
    )
    right_side = velocity_terms + time_step * spec_terms
    right_side = right_side.reshape(3, 2, slot_count, 1, NL * radius_count)
    operator_blocks = inverse_operators.reshape(degree_count, NR, NR // radius_count, radius_count)
    pieces = lax.all_to_all(
        right_side.astype(jnp.bfloat16), "row", split_axis=4, concat_axis=3, tiled=True
    ).astype(right_side.dtype)
    field_count = pieces.shape[0]
    columns = pieces.reshape(
        field_count, 2, slot_count, NR // radius_count, degree_count, radius_count
    )
    return jnp.einsum(
        "cpsqlr,laqr->cpsla", columns, operator_blocks, precision=lax.Precision.HIGHEST
    )


def solution(mesh):
    in_specs = (
        P(None, None, "ma", "row", None),
        P(None, None, "ma", "row", None),
        P(),
        P("ma", None, None),
        P("ma", None, None),
        P("row", None, None),
    )
    out_specs = P(None, None, "ma", "row", None)
    return jax.shard_map(
        per_device, mesh=mesh, in_specs=in_specs, out_specs=out_specs, check_vma=False
    )
```

```python
import functools
import math

import jax
import jax.numpy as jnp
from jax import lax
from jax.experimental import pallas as pl
from jax.experimental.pallas import tpu as pltpu
from jax.sharding import PartitionSpec as P

NL = 384
NLAT = 576
NLON = 1152
NR = 128


LANES = 128
ROWS = 16
QUAD = 4


time_step = 0.5
rotation = 2.0


def longitude_table(orders):
    points = jnp.arange(NLON, dtype=jnp.int32)
    phases = orders[:, None] * points[None, :] % NLON
    angles = phases.astype(jnp.float32) * (2.0 * math.pi / NLON)
    return jnp.stack([jnp.cos(angles), -jnp.sin(angles)]).astype(jnp.bfloat16)


def cross_terms(moving, spinning):
    spin_total = spinning[2] + rotation
    component_one = moving[1] * spin_total - moving[2] * spinning[1]
    component_two = moving[2] * spinning[0] - moving[0] * spin_total
    component_three = moving[0] * spinning[1] - moving[1] * spinning[0]
    return component_one, component_two, component_three


def synth_kernel(scale_ref, spec_ref, table_ref, early_ref, late_ref, turned):
    comps, parts, slots, radii, degrees = spec_ref.shape
    lat = table_ref.shape[1]
    half = radii // 2
    rows = comps * parts * half
    first_slot = pl.program_id(0) * slots
    for s in range(slots):
        spec = spec_ref[:, :, s].reshape(2 * rows, degrees)
        sums = lax.dot_general(
            spec, table_ref[s], (((1,), (1,)), ((), ())), preferred_element_type=jnp.float32
        )
        sums = (sums * scale_ref[first_slot + s]).reshape(comps * parts, 2, half, lat)
        wide = jnp.concatenate(
            [sums[:, 0].reshape(rows, lat), sums[:, 1].reshape(rows, lat)], axis=1
        )
        for t in range(2 * lat // LANES):
            turned[t, pl.ds(s, rows, stride=slots), :] = wide[:, t * LANES : (t + 1) * LANES]
    owners = half // 2
    for i in range(comps * parts):
        c, p = i // parts, i % parts
        for h, out_ref in enumerate((early_ref, late_ref)):
            for d in range(owners):
                row = (i * half + h * owners + d) * slots
                for t in range(2 * lat // LANES):
                    out_ref[d, c, p, :, t * LANES : (t + 1) * LANES] = turned[
                        t, pl.ds(row, slots), :
                    ].astype(jnp.bfloat16)


def synthesize(spec, table, scale):
    comps, parts, slots, radii, degrees = spec.shape
    lat = table.shape[1]
    owners = radii // 4
    shape = jax.ShapeDtypeStruct((owners, comps, parts, slots, 2 * lat), jnp.bfloat16)
    out_spec = pl.BlockSpec((owners, comps, parts, ROWS, 2 * lat), lambda i: (0, 0, 0, i, 0))
    rows = comps * parts * radii // 2 * ROWS
    return pl.pallas_call(
        synth_kernel,
        grid=(slots // ROWS,),
        in_specs=[
            pl.BlockSpec(memory_space=pltpu.SMEM),
            pl.BlockSpec((comps, parts, ROWS, radii, degrees), lambda i: (0, 0, i, 0, 0)),
            pl.BlockSpec((ROWS, lat, degrees), lambda i: (i, 0, 0)),
        ],
        out_specs=[out_spec, out_spec],
        out_shape=[shape, shape],
        scratch_shapes=[pltpu.VMEM((2 * lat // LANES, rows, LANES), jnp.float32)],
        compiler_params=pltpu.CompilerParams(vmem_limit_bytes=56 << 20),
        cost_estimate=pl.CostEstimate(
            flops=2 * spec.size * lat,
            bytes_accessed=2 * (spec.size + table.size + spec.size * lat // degrees),
            transcendentals=0,
        ),
    )(scale, spec, table)


def grid_kernel(scale, move_ref, spin_ref, across_ref, along_ref, out_ref, packed, total):
    owners, comps, parts, slots, wide = move_ref.shape
    waves = owners * parts * slots
    points = along_ref.shape[1]
    for c in range(comps):
        packed[:, c * wide : (c + 1) * wide] = move_ref[:, c].reshape(waves, wide)
        packed[:, (comps + c) * wide : (comps + c + 1) * wide] = spin_ref[:, c].reshape(waves, wide)
    step = points // 3
    for k in range(3):
        grid = jnp.dot(
            across_ref[k * step : (k + 1) * step, :],
            packed[...],
            preferred_element_type=jnp.float32,
        )
        fields = [grid[:, i * wide : (i + 1) * wide] for i in range(2 * comps)]
        products = jnp.concatenate(cross_terms(fields[:3], fields[3:]), axis=1)
        part = jnp.dot(
            along_ref[:, k * step : (k + 1) * step],
            products.astype(jnp.bfloat16),
            preferred_element_type=jnp.float32,
        )
        total[...] = part if k == 0 else total[...] + part
    for c in range(comps):
        back = (scale * total[:, c * wide : (c + 1) * wide]).astype(jnp.bfloat16)
        out_ref[:, c] = back.reshape(owners, parts, slots, wide)


def through_grid(moving, spinning, across, along, scale):
    owners, comps, parts, slots, columns = moving.shape
    waves, points = along.shape
    wide = columns // 3
    block = pl.BlockSpec((owners, comps, parts, slots, wide), lambda i: (0, 0, 0, 0, i))
    return pl.pallas_call(
        functools.partial(grid_kernel, scale),
        grid=(columns // wide,),
        in_specs=[
            block,
            block,
            pl.BlockSpec((points, waves), lambda i: (0, 0)),
            pl.BlockSpec((waves, points), lambda i: (0, 0)),
        ],
        out_specs=block,
        out_shape=jax.ShapeDtypeStruct(moving.shape, jnp.bfloat16),
        scratch_shapes=[
            pltpu.VMEM((waves, 2 * comps * wide), jnp.bfloat16),
            pltpu.VMEM((waves, comps * wide), jnp.float32),
        ],
        compiler_params=pltpu.CompilerParams(vmem_limit_bytes=56 << 20),
        cost_estimate=pl.CostEstimate(
            flops=2 * 3 * comps * waves * points * columns,
            bytes_accessed=6 * moving.size,
            transcendentals=0,
        ),
    )(moving, spinning, across, along)


def analyze_kernel(h, in_ref, table_ref, velocity_ref, out_ref, turned):
    comps, parts, slots, radii, degrees = velocity_ref.shape
    lat = table_ref.shape[1]
    owners = in_ref.shape[0]
    rows = comps * parts * owners
    tiles = 2 * lat // LANES
    for i in range(comps * parts):
        for d in range(owners):
            row = (i * owners + d) * slots
            for t in range(tiles):
                turned[t, pl.ds(row, slots), :] = in_ref[
                    d, i // parts, i % parts, :, t * LANES : (t + 1) * LANES
                ].astype(jnp.float32)
    groups, own = out_ref.shape[0], out_ref.shape[2]
    for quad in range(slots // QUAD):
        sides = []
        for s in range(quad * QUAD, (quad + 1) * QUAD):
            wide = jnp.concatenate(
                [turned[t, pl.ds(s, rows, stride=slots), :] for t in range(tiles)], axis=1
            )
            pieces = [wide[:, :lat], wide[:, lat:]]
            pieces = [x.reshape(comps * parts, 1, owners, lat) for x in pieces]
            left = jnp.concatenate(pieces, axis=1).reshape(2 * rows, lat)
            terms = jnp.dot(
                left.astype(jnp.bfloat16), table_ref[s], preferred_element_type=jnp.float32
            )
            moving = velocity_ref[:, :, s].astype(jnp.float32)
            moving = moving.reshape(comps * parts, 2, 2, owners, degrees)[:, :, h]
            sides.append(moving.reshape(2 * rows, degrees) + time_step * terms)
        turned_sides = jnp.concatenate(sides, axis=0).T.astype(jnp.bfloat16)
        for g in range(groups):
            out_ref[g, quad] = turned_sides[g * own : (g + 1) * own]


def analyze(h, back, table, velocity, groups):
    comps, parts, slots, radii, degrees = velocity.shape
    lat = table.shape[1]
    owners = back.shape[0]
    own = degrees // groups
    wide = QUAD * comps * parts * 2 * owners
    rows = comps * parts * owners * ROWS
    return pl.pallas_call(
        functools.partial(analyze_kernel, h),
        grid=(slots // ROWS,),
        in_specs=[
            pl.BlockSpec((owners, comps, parts, ROWS, 2 * lat), lambda i: (0, 0, 0, i, 0)),
            pl.BlockSpec((ROWS, lat, degrees), lambda i: (i, 0, 0)),
            pl.BlockSpec((comps, parts, ROWS, radii, degrees), lambda i: (0, 0, i, 0, 0)),
        ],
        out_specs=pl.BlockSpec((groups, ROWS // QUAD, own, wide), lambda i: (0, i, 0, 0)),
        out_shape=jax.ShapeDtypeStruct((groups, slots // QUAD, own, wide), jnp.bfloat16),
        scratch_shapes=[pltpu.VMEM((2 * lat // LANES, rows, LANES), jnp.float32)],
        compiler_params=pltpu.CompilerParams(vmem_limit_bytes=56 << 20),
        cost_estimate=pl.CostEstimate(
            flops=velocity.size * lat,
            bytes_accessed=2 * (3 * velocity.size + table.size),
            transcendentals=0,
        ),
    )(back, table, velocity)


def radial_kernel(early_ref, late_ref, order_ref, operator_ref, out_ref, lines):
    groups, quads, own, wide = early_ref.shape
    comps, parts, slots = out_ref.shape[:3]
    full = out_ref.shape[4]
    sets = 2 * groups
    for u in range(wide // LANES):
        halves = [
            ref[z, :, :, u * LANES : (u + 1) * LANES].reshape(quads * own, LANES)
            for z in range(groups)
            for ref in (early_ref, late_ref)
        ]
        packed = jnp.concatenate(halves, axis=1)
        sorted_lines = jnp.dot(packed, order_ref[...], preferred_element_type=jnp.float32)
        for g in range(sets):
            row = (u * sets + g) * quads * own
            lines[pl.ds(row, quads * own), :] = sorted_lines[:, g * full : (g + 1) * full]
    count = comps * parts * slots
    for degree in range(own):
        left = lines[pl.ds(degree, count, stride=own), :].astype(jnp.bfloat16)
        lines[pl.ds(degree, count, stride=own), :] = lax.dot_general(
            left,
            operator_ref[degree],
            (((1,), (1,)), ((), ())),
            preferred_element_type=jnp.float32,
        )
    for s in range(slots):
        for i in range(comps * parts):
            row = ((s % QUAD * comps * parts + i) * quads + s // QUAD) * own
            out_ref[i // parts, i % parts, s] = lines[pl.ds(row, own), :]


def radial_order(groups, owners, full):
    sets = LANES // (2 * owners)
    lane = jnp.arange(2 * groups * LANES, dtype=jnp.int32)
    d, k = lane % owners, lane // owners % 2
    g = lane // (2 * owners) % sets
    h, z = lane // LANES % 2, lane // (2 * LANES)
    target = g * full + ((z * 2 + k) * 2 + h) * owners + d
    columns = jnp.arange(sets * full, dtype=jnp.int32)
    return (target[:, None] == columns[None, :]).astype(jnp.bfloat16)


def radial_solve(early, late, operators, comps, parts, slots, owners):
    groups, quads, own, wide = early.shape
    full = operators.shape[1]
    order = radial_order(groups, owners, full)
    block = pl.BlockSpec((groups, ROWS // QUAD, own, wide), lambda i: (0, i, 0, 0))
    return pl.pallas_call(
        radial_kernel,
        grid=(slots // ROWS,),
        in_specs=[
            block,
            block,
            pl.BlockSpec(order.shape, lambda i: (0, 0)),
            pl.BlockSpec(operators.shape, lambda i: (0, 0, 0)),
        ],
        out_specs=pl.BlockSpec((comps, parts, ROWS, own, full), lambda i: (0, 0, i, 0, 0)),
        out_shape=jax.ShapeDtypeStruct((comps, parts, slots, own, full), jnp.float32),
        scratch_shapes=[pltpu.VMEM((comps * parts * ROWS * own, LANES), jnp.float32)],
        compiler_params=pltpu.CompilerParams(vmem_limit_bytes=56 << 20),
        cost_estimate=pl.CostEstimate(
            flops=4 * early.size * order.shape[0],
            bytes_accessed=12 * early.size,
            transcendentals=0,
        ),
    )(early, late, order, operators)


def fits(velocity, legendre_bf, owners, groups):
    comps, parts, slots, radii, degrees = velocity.shape
    return (
        groups * radii == LANES
        and LANES % (2 * owners) == 0
        and owners % 8 == 0
        and QUAD * comps * parts * 2 * owners % LANES == 0
        and degrees % (groups * ROWS) == 0
        and velocity.shape[3] == 4 * owners
        and velocity.shape[3] % (2 * ROWS) == 0
        and velocity.shape[2] % ROWS == 0
        and (2 * legendre_bf.shape[2]) % (3 * LANES) == 0
    )


def by_radius(velocity, vorticity, order_table, legendre_bf, weighted, inverse_operators):
    owners = lax.axis_size("ma")
    slots = velocity.shape[2]
    own_orders = lax.dynamic_slice_in_dim(order_table, lax.axis_index("ma") * slots, slots)
    scale = jnp.where(own_orders == 0, 1.0, 2.0).astype(jnp.float32) / NL

    def exchange(x):
        return lax.all_to_all(x, "ma", split_axis=0, concat_axis=0, tiled=True)

    legendre = jnp.transpose(legendre_bf, (0, 2, 1))
    weights = jnp.transpose(weighted, (0, 2, 1))
    move_early, move_late = synthesize(velocity, legendre, scale)
    spin_early, spin_late = synthesize(vorticity, legendre, scale)
    move_early, spin_early = exchange(move_early), exchange(spin_early)
    move_late, spin_late = exchange(move_late), exchange(spin_late)
    table = longitude_table(order_table).reshape(2, owners, slots, NLON)
    along = jnp.transpose(table, (1, 0, 2, 3)).reshape(2 * owners * slots, NLON)
    across = jnp.transpose(along)
    early = exchange(through_grid(move_early, spin_early, across, along, NL / NLON))
    late = exchange(through_grid(move_late, spin_late, across, along, NL / NLON))
    groups = lax.axis_size("row")
    sides = [
        lax.all_to_all(
            analyze(h, back, weights, velocity, groups),
            "row",
            split_axis=0,
            concat_axis=0,
            tiled=True,
        )
        for h, back in enumerate((early, late))
    ]
    operators = inverse_operators.astype(jnp.bfloat16)
    return radial_solve(*sides, operators, *velocity.shape[:3], owners)


def per_device(velocity, vorticity, order_table, legendre_bf, weighted, inverse_operators):
    if fits(velocity, legendre_bf, lax.axis_size("ma"), lax.axis_size("row")):
        return by_radius(
            velocity, vorticity, order_table, legendre_bf, weighted, inverse_operators
        )
    slot_count = velocity.shape[2]
    radius_count = velocity.shape[3]
    degree_count = inverse_operators.shape[0]
    own_orders = lax.dynamic_slice_in_dim(
        order_table, lax.axis_index("ma") * slot_count, slot_count
    )
    own_scale = jnp.where(own_orders == 0, 1.0, 2.0).astype(jnp.float32) / NL
    harmonics = longitude_table(order_table)

    def arrange(grid_values):
        scaled = (grid_values * own_scale[None, None, :, None, None]).astype(jnp.bfloat16)
        ordered = jnp.transpose(scaled, (0, 1, 2, 4, 3))
        return ordered.reshape(3, 2, slot_count, NLAT * radius_count)

    def synthesize(spectral):
        grid_values = jnp.einsum(
            "cpsrl,slt->cpsrt", spectral, legendre_bf, preferred_element_type=jnp.float32
        )
        return arrange(grid_values)

    def to_longitude(pieces):
        return jnp.einsum("cpsk,psn->ckn", pieces, harmonics, preferred_element_type=jnp.float32)

    velocity_grid = to_longitude(
        lax.all_to_all(synthesize(velocity), "ma", split_axis=3, concat_axis=2, tiled=True)
    )
    vorticity_grid = to_longitude(
        lax.all_to_all(synthesize(vorticity), "ma", split_axis=3, concat_axis=2, tiled=True)
    )
    products = jnp.stack(cross_terms(velocity_grid, vorticity_grid)).astype(jnp.bfloat16)
    spectral_back = jnp.einsum(
        "ckn,psn->cpsk", products, harmonics, preferred_element_type=jnp.float32
    )
    spectral_back = (NL / NLON * spectral_back).astype(jnp.bfloat16)
    pieces = lax.all_to_all(spectral_back, "ma", split_axis=2, concat_axis=3, tiled=True)
    field_count = pieces.shape[0]
    split_pieces = pieces.reshape(field_count, 2, slot_count, NLAT, radius_count)
    terms = jnp.einsum(
        "cpstr,slt->cpslr", split_pieces, weighted, preferred_element_type=jnp.float32
    )
    spec_terms = terms.reshape(field_count, 2, slot_count, NL * radius_count)
    velocity_terms = jnp.transpose(velocity.astype(jnp.float32), (0, 1, 2, 4, 3)).reshape(
        3, 2, slot_count, NL * radius_count
    )
    right_side = velocity_terms + time_step * spec_terms
    right_side = right_side.reshape(3, 2, slot_count, 1, NL * radius_count)
    operator_blocks = inverse_operators.reshape(degree_count, NR, NR // radius_count, radius_count)
    pieces = lax.all_to_all(
        right_side.astype(jnp.bfloat16), "row", split_axis=4, concat_axis=3, tiled=True
    ).astype(right_side.dtype)
    field_count = pieces.shape[0]
    columns = pieces.reshape(
        field_count, 2, slot_count, NR // radius_count, degree_count, radius_count
    )
    return jnp.einsum(
        "cpsqlr,laqr->cpsla", columns, operator_blocks, precision=lax.Precision.HIGHEST
    )


def solution(mesh):
    in_specs = (
        P(None, None, "ma", "row", None),
        P(None, None, "ma", "row", None),
        P(),
        P("ma", None, None),
        P("ma", None, None),
        P("row", None, None),
    )
    out_specs = P(None, None, "ma", "row", None)
    return jax.shard_map(
        per_device, mesh=mesh, in_specs=in_specs, out_specs=out_specs, check_vma=False
    )
```

```python
import functools
import math

import jax
import jax.numpy as jnp
from jax import lax
from jax.experimental import pallas as pl
from jax.experimental.pallas import tpu as pltpu
from jax.sharding import PartitionSpec as P

NL = 384
NLAT = 576
NLON = 1152
NR = 128


LANES = 128
ROWS = 16
QUAD = 4


time_step = 0.5
rotation = 2.0


def longitude_table(orders):
    points = jnp.arange(NLON, dtype=jnp.int32)
    phases = orders[:, None] * points[None, :] % NLON
    angles = phases.astype(jnp.float32) * (2.0 * math.pi / NLON)
    return jnp.stack([jnp.cos(angles), -jnp.sin(angles)]).astype(jnp.bfloat16)


def cross_terms(moving, spinning):
    spin_total = spinning[2] + rotation
    component_one = moving[1] * spin_total - moving[2] * spinning[1]
    component_two = moving[2] * spinning[0] - moving[0] * spin_total
    component_three = moving[0] * spinning[1] - moving[1] * spinning[0]
    return component_one, component_two, component_three


def synth_kernel(scale_ref, spec_ref, table_ref, early_ref, late_ref, turned):
    comps, parts, slots, radii, degrees = spec_ref.shape
    lat = table_ref.shape[1]
    half = radii // 2
    rows = comps * parts * half
    first_slot = pl.program_id(0) * slots
    for s in range(slots):
        spec = spec_ref[:, :, s].reshape(2 * rows, degrees)
        sums = lax.dot_general(
            spec, table_ref[s], (((1,), (1,)), ((), ())), preferred_element_type=jnp.float32
        )
        sums = (sums * scale_ref[first_slot + s]).reshape(comps * parts, 2, half, lat)
        wide = jnp.concatenate(
            [sums[:, 0].reshape(rows, lat), sums[:, 1].reshape(rows, lat)], axis=1
        )
        for t in range(2 * lat // LANES):
            turned[t, pl.ds(s, rows, stride=slots), :] = wide[:, t * LANES : (t + 1) * LANES]
    owners = half // 2
    for i in range(comps * parts):
        c, p = i // parts, i % parts
        for h, out_ref in enumerate((early_ref, late_ref)):
            for d in range(owners):
                row = (i * half + h * owners + d) * slots
                for t in range(2 * lat // LANES):
                    out_ref[d, c, p, :, t * LANES : (t + 1) * LANES] = turned[
                        t, pl.ds(row, slots), :
                    ].astype(jnp.bfloat16)


def synthesize(spec, table, scale):
    comps, parts, slots, radii, degrees = spec.shape
    lat = table.shape[1]
    owners = radii // 4
    shape = jax.ShapeDtypeStruct((owners, comps, parts, slots, 2 * lat), jnp.bfloat16)
    out_spec = pl.BlockSpec((owners, comps, parts, ROWS, 2 * lat), lambda i: (0, 0, 0, i, 0))
    rows = comps * parts * radii // 2 * ROWS
    return pl.pallas_call(
        synth_kernel,
        grid=(slots // ROWS,),
        in_specs=[
            pl.BlockSpec(memory_space=pltpu.SMEM),
            pl.BlockSpec((comps, parts, ROWS, radii, degrees), lambda i: (0, 0, i, 0, 0)),
            pl.BlockSpec((ROWS, lat, degrees), lambda i: (i, 0, 0)),
        ],
        out_specs=[out_spec, out_spec],
        out_shape=[shape, shape],
        scratch_shapes=[pltpu.VMEM((2 * lat // LANES, rows, LANES), jnp.float32)],
        compiler_params=pltpu.CompilerParams(vmem_limit_bytes=56 << 20),
        cost_estimate=pl.CostEstimate(
            flops=2 * spec.size * lat,
            bytes_accessed=2 * (spec.size + table.size + spec.size * lat // degrees),
            transcendentals=0,
        ),
    )(scale, spec, table)


def grid_kernel(scale, move_ref, spin_ref, across_ref, along_ref, out_ref, packed, total):
    owners, comps, parts, slots, wide = move_ref.shape
    waves = owners * parts * slots
    points = along_ref.shape[1]
    for c in range(comps):
        packed[:, c * wide : (c + 1) * wide] = move_ref[:, c].reshape(waves, wide)
        packed[:, (comps + c) * wide : (comps + c + 1) * wide] = spin_ref[:, c].reshape(waves, wide)
    step = points // 3
    for k in range(3):
        grid = jnp.dot(
            across_ref[k * step : (k + 1) * step, :],
            packed[...],
            preferred_element_type=jnp.float32,
        )
        fields = [grid[:, i * wide : (i + 1) * wide] for i in range(2 * comps)]
        products = jnp.concatenate(cross_terms(fields[:3], fields[3:]), axis=1)
        part = jnp.dot(
            along_ref[:, k * step : (k + 1) * step],
            products.astype(jnp.bfloat16),
            preferred_element_type=jnp.float32,
        )
        total[...] = part if k == 0 else total[...] + part
    for c in range(comps):
        back = (scale * total[:, c * wide : (c + 1) * wide]).astype(jnp.bfloat16)
        out_ref[:, c] = back.reshape(owners, parts, slots, wide)


def through_grid(moving, spinning, across, along, scale):
    owners, comps, parts, slots, columns = moving.shape
    waves, points = along.shape
    wide = columns // 3
    block = pl.BlockSpec((owners, comps, parts, slots, wide), lambda i: (0, 0, 0, 0, i))
    return pl.pallas_call(
        functools.partial(grid_kernel, scale),
        grid=(columns // wide,),
        in_specs=[
            block,
            block,
            pl.BlockSpec((points, waves), lambda i: (0, 0)),
            pl.BlockSpec((waves, points), lambda i: (0, 0)),
        ],
        out_specs=block,
        out_shape=jax.ShapeDtypeStruct(moving.shape, jnp.bfloat16),
        scratch_shapes=[
            pltpu.VMEM((waves, 2 * comps * wide), jnp.bfloat16),
            pltpu.VMEM((waves, comps * wide), jnp.float32),
        ],
        compiler_params=pltpu.CompilerParams(vmem_limit_bytes=56 << 20),
        cost_estimate=pl.CostEstimate(
            flops=2 * 3 * comps * waves * points * columns,
            bytes_accessed=6 * moving.size,
            transcendentals=0,
        ),
    )(moving, spinning, across, along)


def analyze_kernel(h, in_ref, table_ref, velocity_ref, out_ref, turned):
    comps, parts, slots, radii, degrees = velocity_ref.shape
    lat = table_ref.shape[1]
    owners = in_ref.shape[0]
    rows = comps * parts * owners
    tiles = 2 * lat // LANES
    for i in range(comps * parts):
        for d in range(owners):
            row = (i * owners + d) * slots
            for t in range(tiles):
                turned[t, pl.ds(row, slots), :] = in_ref[
                    d, i // parts, i % parts, :, t * LANES : (t + 1) * LANES
                ].astype(jnp.float32)
    groups, own = out_ref.shape[0], out_ref.shape[2]
    for quad in range(slots // QUAD):
        sides = []
        for s in range(quad * QUAD, (quad + 1) * QUAD):
            wide = jnp.concatenate(
                [turned[t, pl.ds(s, rows, stride=slots), :] for t in range(tiles)], axis=1
            )
            pieces = [wide[:, :lat], wide[:, lat:]]
            pieces = [x.reshape(comps * parts, 1, owners, lat) for x in pieces]
            left = jnp.concatenate(pieces, axis=1).reshape(2 * rows, lat)
            terms = jnp.dot(
                left.astype(jnp.bfloat16), table_ref[s], preferred_element_type=jnp.float32
            )
            moving = velocity_ref[:, :, s].astype(jnp.float32)
            moving = moving.reshape(comps * parts, 2, 2, owners, degrees)[:, :, h]
            sides.append(moving.reshape(2 * rows, degrees) + time_step * terms)
        turned_sides = jnp.concatenate(sides, axis=0).T.astype(jnp.bfloat16)
        for g in range(groups):
            out_ref[g, quad] = turned_sides[g * own : (g + 1) * own]


def analyze(h, back, table, velocity, groups):
    comps, parts, slots, radii, degrees = velocity.shape
    lat = table.shape[1]
    owners = back.shape[0]
    own = degrees // groups
    wide = QUAD * comps * parts * 2 * owners
    rows = comps * parts * owners * ROWS
    return pl.pallas_call(
        functools.partial(analyze_kernel, h),
        grid=(slots // ROWS,),
        in_specs=[
            pl.BlockSpec((owners, comps, parts, ROWS, 2 * lat), lambda i: (0, 0, 0, i, 0)),
            pl.BlockSpec((ROWS, lat, degrees), lambda i: (i, 0, 0)),
            pl.BlockSpec((comps, parts, ROWS, radii, degrees), lambda i: (0, 0, i, 0, 0)),
        ],
        out_specs=pl.BlockSpec((groups, ROWS // QUAD, own, wide), lambda i: (0, i, 0, 0)),
        out_shape=jax.ShapeDtypeStruct((groups, slots // QUAD, own, wide), jnp.bfloat16),
        scratch_shapes=[pltpu.VMEM((2 * lat // LANES, rows, LANES), jnp.float32)],
        compiler_params=pltpu.CompilerParams(vmem_limit_bytes=56 << 20),
        cost_estimate=pl.CostEstimate(
            flops=velocity.size * lat,
            bytes_accessed=2 * (3 * velocity.size + table.size),
            transcendentals=0,
        ),
    )(back, table, velocity)


def radial_kernel(*refs):
    *piece_refs, order_ref, operator_ref, out_ref, lines, solved = refs
    quads, own, wide = piece_refs[0].shape
    comps, parts, slots = out_ref.shape[:3]
    full = out_ref.shape[4]
    sets = len(piece_refs)
    for u in range(wide // LANES):
        packed = jnp.concatenate(
            [
                ref[:, :, u * LANES : (u + 1) * LANES].reshape(quads * own, LANES)
                for ref in piece_refs
            ],
            axis=1,
        )
        sorted_lines = jnp.dot(packed, order_ref[...], preferred_element_type=jnp.float32)
        for g in range(sets):
            row = (u * sets + g) * quads * own
            lines[pl.ds(row, quads * own), :] = sorted_lines[:, g * full : (g + 1) * full]
    count = comps * parts * slots
    for degree in range(own):
        left = lines[pl.ds(degree, count, stride=own), :].astype(jnp.bfloat16)
        solved[pl.ds(degree, count, stride=own), :] = jnp.dot(
            left, operator_ref[degree], preferred_element_type=jnp.float32
        )
    for s in range(slots):
        for i in range(comps * parts):
            row = ((s % QUAD * comps * parts + i) * quads + s // QUAD) * own
            out_ref[i // parts, i % parts, s] = solved[pl.ds(row, own), :]


def radial_order(groups, owners, full, me):
    sets = LANES // (2 * owners)
    lane = jnp.arange(2 * groups * LANES, dtype=jnp.int32)
    d, k = lane % owners, lane // owners % 2
    g = lane // (2 * owners) % sets
    step, h = lane // LANES % groups, lane // (LANES * groups)
    z = (me - step + groups) % groups
    target = g * full + ((z * 2 + k) * 2 + h) * owners + d
    columns = jnp.arange(sets * full, dtype=jnp.int32)
    return (target[:, None] == columns[None, :]).astype(jnp.bfloat16)


def radial_solve(pieces, order, operators, comps, parts, slots):
    quads, own, wide = pieces[0].shape
    full = operators.shape[1]
    block = pl.BlockSpec((quads, 2 * ROWS, wide), lambda i: (0, i, 0))
    scratch = pltpu.VMEM((comps * parts * slots * 2 * ROWS, LANES), jnp.float32)
    return pl.pallas_call(
        radial_kernel,
        grid=(own // (2 * ROWS),),
        in_specs=[block] * len(pieces)
        + [
            pl.BlockSpec(order.shape, lambda i: (0, 0)),
            pl.BlockSpec((2 * ROWS, full, full), lambda i: (i, 0, 0)),
        ],
        out_specs=pl.BlockSpec((comps, parts, slots, 2 * ROWS, full), lambda i: (0, 0, 0, i, 0)),
        out_shape=jax.ShapeDtypeStruct((comps, parts, slots, own, full), jnp.float32),
        scratch_shapes=[scratch, scratch],
        compiler_params=pltpu.CompilerParams(vmem_limit_bytes=56 << 20),
        cost_estimate=pl.CostEstimate(
            flops=2 * len(pieces) * pieces[0].size * order.shape[0],
            bytes_accessed=6 * len(pieces) * pieces[0].size,
            transcendentals=0,
        ),
    )(*pieces, order, operators)


def share_degrees(sides, groups):
    me = lax.axis_index("row")
    pieces = []
    for step in range(groups):
        block = lax.dynamic_index_in_dim(sides, (me + step) % groups, keepdims=False)
        if step:
            places = [(i, (i + step) % groups) for i in range(groups)]
            block = lax.ppermute(block, "row", places)
        pieces.append(block)
    return pieces


def fits(velocity, legendre_bf, owners, groups):
    comps, parts, slots, radii, degrees = velocity.shape
    return (
        groups * radii == LANES
        and LANES % (2 * owners) == 0
        and owners % 8 == 0
        and QUAD * comps * parts * 2 * owners % LANES == 0
        and degrees % (groups * 2 * ROWS) == 0
        and velocity.shape[3] == 4 * owners
        and velocity.shape[3] % (2 * ROWS) == 0
        and velocity.shape[2] % ROWS == 0
        and (2 * legendre_bf.shape[2]) % (3 * LANES) == 0
    )


def by_radius(velocity, vorticity, order_table, legendre_bf, weighted, inverse_operators):
    owners = lax.axis_size("ma")
    slots = velocity.shape[2]
    own_orders = lax.dynamic_slice_in_dim(order_table, lax.axis_index("ma") * slots, slots)
    scale = jnp.where(own_orders == 0, 1.0, 2.0).astype(jnp.float32) / NL

    def exchange(x):
        return lax.all_to_all(x, "ma", split_axis=0, concat_axis=0, tiled=True)

    legendre = jnp.transpose(legendre_bf, (0, 2, 1))
    weights = jnp.transpose(weighted, (0, 2, 1))
    move_early, move_late = synthesize(velocity, legendre, scale)
    spin_early, spin_late = synthesize(vorticity, legendre, scale)
    move_early, spin_early = exchange(move_early), exchange(spin_early)
    move_late, spin_late = exchange(move_late), exchange(spin_late)
    table = longitude_table(order_table).reshape(2, owners, slots, NLON)
    along = jnp.transpose(table, (1, 0, 2, 3)).reshape(2 * owners * slots, NLON)
    across = jnp.transpose(along)
    early = exchange(through_grid(move_early, spin_early, across, along, NL / NLON))
    late = exchange(through_grid(move_late, spin_late, across, along, NL / NLON))
    groups = lax.axis_size("row")
    pieces = []
    for h, back in enumerate((early, late)):
        pieces += share_degrees(analyze(h, back, weights, velocity, groups), groups)
    order = radial_order(groups, owners, groups * velocity.shape[3], lax.axis_index("row"))
    operators = jnp.transpose(inverse_operators, (0, 2, 1)).astype(jnp.bfloat16)
    return radial_solve(pieces, order, operators, *velocity.shape[:3])


def per_device(velocity, vorticity, order_table, legendre_bf, weighted, inverse_operators):
    if fits(velocity, legendre_bf, lax.axis_size("ma"), lax.axis_size("row")):
        return by_radius(
            velocity, vorticity, order_table, legendre_bf, weighted, inverse_operators
        )
    slot_count = velocity.shape[2]
    radius_count = velocity.shape[3]
    degree_count = inverse_operators.shape[0]
    own_orders = lax.dynamic_slice_in_dim(
        order_table, lax.axis_index("ma") * slot_count, slot_count
    )
    own_scale = jnp.where(own_orders == 0, 1.0, 2.0).astype(jnp.float32) / NL
    harmonics = longitude_table(order_table)

    def arrange(grid_values):
        scaled = (grid_values * own_scale[None, None, :, None, None]).astype(jnp.bfloat16)
        ordered = jnp.transpose(scaled, (0, 1, 2, 4, 3))
        return ordered.reshape(3, 2, slot_count, NLAT * radius_count)

    def synthesize(spectral):
        grid_values = jnp.einsum(
            "cpsrl,slt->cpsrt", spectral, legendre_bf, preferred_element_type=jnp.float32
        )
        return arrange(grid_values)

    def to_longitude(pieces):
        return jnp.einsum("cpsk,psn->ckn", pieces, harmonics, preferred_element_type=jnp.float32)

    velocity_grid = to_longitude(
        lax.all_to_all(synthesize(velocity), "ma", split_axis=3, concat_axis=2, tiled=True)
    )
    vorticity_grid = to_longitude(
        lax.all_to_all(synthesize(vorticity), "ma", split_axis=3, concat_axis=2, tiled=True)
    )
    products = jnp.stack(cross_terms(velocity_grid, vorticity_grid)).astype(jnp.bfloat16)
    spectral_back = jnp.einsum(
        "ckn,psn->cpsk", products, harmonics, preferred_element_type=jnp.float32
    )
    spectral_back = (NL / NLON * spectral_back).astype(jnp.bfloat16)
    pieces = lax.all_to_all(spectral_back, "ma", split_axis=2, concat_axis=3, tiled=True)
    field_count = pieces.shape[0]
    split_pieces = pieces.reshape(field_count, 2, slot_count, NLAT, radius_count)
    terms = jnp.einsum(
        "cpstr,slt->cpslr", split_pieces, weighted, preferred_element_type=jnp.float32
    )
    spec_terms = terms.reshape(field_count, 2, slot_count, NL * radius_count)
    velocity_terms = jnp.transpose(velocity.astype(jnp.float32), (0, 1, 2, 4, 3)).reshape(
        3, 2, slot_count, NL * radius_count
    )
    right_side = velocity_terms + time_step * spec_terms
    right_side = right_side.reshape(3, 2, slot_count, 1, NL * radius_count)
    operator_blocks = inverse_operators.reshape(degree_count, NR, NR // radius_count, radius_count)
    pieces = lax.all_to_all(
        right_side.astype(jnp.bfloat16), "row", split_axis=4, concat_axis=3, tiled=True
    ).astype(right_side.dtype)
    field_count = pieces.shape[0]
    columns = pieces.reshape(
        field_count, 2, slot_count, NR // radius_count, degree_count, radius_count
    )
    return jnp.einsum(
        "cpsqlr,laqr->cpsla", columns, operator_blocks, precision=lax.Precision.HIGHEST
    )


def solution(mesh):
    in_specs = (
        P(None, None, "ma", "row", None),
        P(None, None, "ma", "row", None),
        P(),
        P("ma", None, None),
        P("ma", None, None),
        P("row", None, None),
    )
    out_specs = P(None, None, "ma", "row", None)
    return jax.shard_map(
        per_device, mesh=mesh, in_specs=in_specs, out_specs=out_specs, check_vma=False
    )
```

```python
import functools
import math

import jax
import jax.numpy as jnp
from jax import lax
from jax.experimental import pallas as pl
from jax.experimental.pallas import tpu as pltpu
from jax.sharding import PartitionSpec as P

NL = 384
NLAT = 576
NLON = 1152
NR = 128


LANES = 128
ROWS = 16
QUAD = 4


time_step = 0.5
rotation = 2.0


def longitude_table(orders):
    points = jnp.arange(NLON, dtype=jnp.int32)
    phases = orders[:, None] * points[None, :] % NLON
    angles = phases.astype(jnp.float32) * (2.0 * math.pi / NLON)
    return jnp.stack([jnp.cos(angles), -jnp.sin(angles)]).astype(jnp.bfloat16)


def cross_terms(moving, spinning):
    spin_total = spinning[2] + rotation
    component_one = moving[1] * spin_total - moving[2] * spinning[1]
    component_two = moving[2] * spinning[0] - moving[0] * spin_total
    component_three = moving[0] * spinning[1] - moving[1] * spinning[0]
    return component_one, component_two, component_three


def synth_kernel(scale_ref, spec_ref, table_ref, early_ref, late_ref, turned):
    comps, parts, slots, radii, degrees = spec_ref.shape
    lat = table_ref.shape[1]
    half = radii // 2
    rows = comps * parts * half
    first_slot = pl.program_id(0) * slots
    for s in range(slots):
        spec = spec_ref[:, :, s].reshape(2 * rows, degrees)
        sums = lax.dot_general(
            spec, table_ref[s], (((1,), (1,)), ((), ())), preferred_element_type=jnp.float32
        )
        sums = (sums * scale_ref[first_slot + s]).reshape(comps * parts, 2, half, lat)
        wide = jnp.concatenate(
            [sums[:, 0].reshape(rows, lat), sums[:, 1].reshape(rows, lat)], axis=1
        )
        for t in range(2 * lat // LANES):
            turned[t, pl.ds(s, rows, stride=slots), :] = wide[:, t * LANES : (t + 1) * LANES]
    owners = half // 2
    for i in range(comps * parts):
        c, p = i // parts, i % parts
        for h, out_ref in enumerate((early_ref, late_ref)):
            for d in range(owners):
                row = (i * half + h * owners + d) * slots
                for t in range(2 * lat // LANES):
                    out_ref[d, c, p, :, t * LANES : (t + 1) * LANES] = turned[
                        t, pl.ds(row, slots), :
                    ].astype(jnp.bfloat16)


def synthesize(spec, table, scale):
    comps, parts, slots, radii, degrees = spec.shape
    lat = table.shape[1]
    owners = radii // 4
    shape = jax.ShapeDtypeStruct((owners, comps, parts, slots, 2 * lat), jnp.bfloat16)
    out_spec = pl.BlockSpec((owners, comps, parts, ROWS, 2 * lat), lambda i: (0, 0, 0, i, 0))
    rows = comps * parts * radii // 2 * ROWS
    return pl.pallas_call(
        synth_kernel,
        grid=(slots // ROWS,),
        in_specs=[
            pl.BlockSpec(memory_space=pltpu.SMEM),
            pl.BlockSpec((comps, parts, ROWS, radii, degrees), lambda i: (0, 0, i, 0, 0)),
            pl.BlockSpec((ROWS, lat, degrees), lambda i: (i, 0, 0)),
        ],
        out_specs=[out_spec, out_spec],
        out_shape=[shape, shape],
        scratch_shapes=[pltpu.VMEM((2 * lat // LANES, rows, LANES), jnp.float32)],
        compiler_params=pltpu.CompilerParams(vmem_limit_bytes=56 << 20),
        cost_estimate=pl.CostEstimate(
            flops=2 * spec.size * lat,
            bytes_accessed=2 * (spec.size + table.size + spec.size * lat // degrees),
            transcendentals=0,
        ),
    )(scale, spec, table)


def grid_kernel(scale, move_ref, spin_ref, across_ref, along_ref, out_ref, packed, total):
    owners, comps, parts, slots, wide = move_ref.shape
    waves = owners * parts * slots
    points = along_ref.shape[1]
    for c in range(comps):
        packed[:, c * wide : (c + 1) * wide] = move_ref[:, c].reshape(waves, wide)
        packed[:, (comps + c) * wide : (comps + c + 1) * wide] = spin_ref[:, c].reshape(waves, wide)
    step = points // 3
    for k in range(3):
        grid = jnp.dot(
            across_ref[k * step : (k + 1) * step, :],
            packed[...],
            preferred_element_type=jnp.float32,
        )
        fields = [grid[:, i * wide : (i + 1) * wide] for i in range(2 * comps)]
        products = jnp.concatenate(cross_terms(fields[:3], fields[3:]), axis=1)
        part = jnp.dot(
            along_ref[:, k * step : (k + 1) * step],
            products.astype(jnp.bfloat16),
            preferred_element_type=jnp.float32,
        )
        total[...] = part if k == 0 else total[...] + part
    for c in range(comps):
        back = (scale * total[:, c * wide : (c + 1) * wide]).astype(jnp.bfloat16)
        out_ref[:, c] = back.reshape(owners, parts, slots, wide)


def through_grid(moving, spinning, across, along, scale):
    owners, comps, parts, slots, columns = moving.shape
    waves, points = along.shape
    wide = columns // 3
    block = pl.BlockSpec((owners, comps, parts, slots, wide), lambda i: (0, 0, 0, 0, i))
    return pl.pallas_call(
        functools.partial(grid_kernel, scale),
        grid=(columns // wide,),
        in_specs=[
            block,
            block,
            pl.BlockSpec((points, waves), lambda i: (0, 0)),
            pl.BlockSpec((waves, points), lambda i: (0, 0)),
        ],
        out_specs=block,
        out_shape=jax.ShapeDtypeStruct(moving.shape, jnp.bfloat16),
        scratch_shapes=[
            pltpu.VMEM((waves, 2 * comps * wide), jnp.bfloat16),
            pltpu.VMEM((waves, comps * wide), jnp.float32),
        ],
        compiler_params=pltpu.CompilerParams(vmem_limit_bytes=56 << 20),
        cost_estimate=pl.CostEstimate(
            flops=2 * 3 * comps * waves * points * columns,
            bytes_accessed=6 * moving.size,
            transcendentals=0,
        ),
    )(moving, spinning, across, along)


def analyze_kernel(h, in_ref, table_ref, velocity_ref, out_ref, turned):
    comps, parts, slots, radii, degrees = velocity_ref.shape
    lat = table_ref.shape[1]
    owners = in_ref.shape[0]
    rows = comps * parts * owners
    tiles = 2 * lat // LANES
    for i in range(comps * parts):
        for d in range(owners):
            row = (i * owners + d) * slots
            for t in range(tiles):
                turned[t, pl.ds(row, slots), :] = in_ref[
                    d, i // parts, i % parts, :, t * LANES : (t + 1) * LANES
                ].astype(jnp.float32)
    groups, own = out_ref.shape[0], out_ref.shape[2]
    for quad in range(slots // QUAD):
        sides = []
        for s in range(quad * QUAD, (quad + 1) * QUAD):
            wide = jnp.concatenate(
                [turned[t, pl.ds(s, rows, stride=slots), :] for t in range(tiles)], axis=1
            )
            pieces = [wide[:, :lat], wide[:, lat:]]
            pieces = [x.reshape(comps * parts, 1, owners, lat) for x in pieces]
            left = jnp.concatenate(pieces, axis=1).reshape(2 * rows, lat)
            terms = jnp.dot(
                left.astype(jnp.bfloat16), table_ref[s], preferred_element_type=jnp.float32
            )
            moving = velocity_ref[:, :, s].astype(jnp.float32)
            moving = moving.reshape(comps * parts, 2, 2, owners, degrees)[:, :, h]
            sides.append(moving.reshape(2 * rows, degrees) + time_step * terms)
        turned_sides = jnp.concatenate(sides, axis=0).T.astype(jnp.bfloat16)
        for g in range(groups):
            out_ref[g, quad] = turned_sides[g * own : (g + 1) * own]


def analyze(h, back, table, velocity, groups):
    comps, parts, slots, radii, degrees = velocity.shape
    lat = table.shape[1]
    owners = back.shape[0]
    own = degrees // groups
    wide = QUAD * comps * parts * 2 * owners
    rows = comps * parts * owners * ROWS
    return pl.pallas_call(
        functools.partial(analyze_kernel, h),
        grid=(slots // ROWS,),
        in_specs=[
            pl.BlockSpec((owners, comps, parts, ROWS, 2 * lat), lambda i: (0, 0, 0, i, 0)),
            pl.BlockSpec((ROWS, lat, degrees), lambda i: (i, 0, 0)),
            pl.BlockSpec((comps, parts, ROWS, radii, degrees), lambda i: (0, 0, i, 0, 0)),
        ],
        out_specs=pl.BlockSpec((groups, ROWS // QUAD, own, wide), lambda i: (0, i, 0, 0)),
        out_shape=jax.ShapeDtypeStruct((groups, slots // QUAD, own, wide), jnp.bfloat16),
        scratch_shapes=[pltpu.VMEM((2 * lat // LANES, rows, LANES), jnp.float32)],
        compiler_params=pltpu.CompilerParams(vmem_limit_bytes=56 << 20),
        cost_estimate=pl.CostEstimate(
            flops=velocity.size * lat,
            bytes_accessed=2 * (3 * velocity.size + table.size),
            transcendentals=0,
        ),
    )(back, table, velocity)


def radial_kernel(begun, *refs):
    refs = refs[1:] if begun else refs
    *piece_refs, order_ref, operator_ref, out_ref, lines, solved = refs
    quads, own, wide = piece_refs[0].shape
    comps, parts, slots = out_ref.shape[:3]
    full = out_ref.shape[4]
    sets = len(piece_refs)
    for u in range(wide // LANES):
        packed = jnp.concatenate(
            [
                ref[:, :, u * LANES : (u + 1) * LANES].reshape(quads * own, LANES)
                for ref in piece_refs
            ],
            axis=1,
        )
        sorted_lines = jnp.dot(packed, order_ref[...], preferred_element_type=jnp.float32)
        for g in range(sets):
            row = (u * sets + g) * quads * own
            lines[pl.ds(row, quads * own), :] = sorted_lines[:, g * full : (g + 1) * full]
    count = comps * parts * slots
    for degree in range(own):
        left = lines[pl.ds(degree, count, stride=own), :].astype(jnp.bfloat16)
        solved[pl.ds(degree, count, stride=own), :] = jnp.dot(
            left, operator_ref[degree], preferred_element_type=jnp.float32
        )
    for s in range(slots):
        for i in range(comps * parts):
            row = ((s % QUAD * comps * parts + i) * quads + s // QUAD) * own
            out_ref[i // parts, i % parts, s] = solved[pl.ds(row, own), :]


def radial_order(groups, owners, full, me):
    sets = LANES // (2 * owners)
    lane = jnp.arange(2 * groups * LANES, dtype=jnp.int32)
    d, k = lane % owners, lane // owners % 2
    g = lane // (2 * owners) % sets
    step, h = lane // LANES % groups, lane // (LANES * groups)
    z = (me - step + groups) % groups
    target = g * full + ((z * 2 + k) * 2 + h) * owners + d
    columns = jnp.arange(sets * full, dtype=jnp.int32)
    return (target[:, None] == columns[None, :]).astype(jnp.bfloat16)


def radial_solve(pieces, order, operators, comps, parts, slots, part, done):
    quads, own, wide = pieces[0].shape
    begun = [] if done is None else [done]
    full = operators.shape[1]
    block = pl.BlockSpec((quads, 2 * ROWS, wide), lambda i: (0, i, 0))
    scratch = pltpu.VMEM((comps * parts * quads * QUAD * 2 * ROWS, LANES), jnp.float32)
    return pl.pallas_call(
        functools.partial(radial_kernel, bool(begun)),
        grid=(own // (2 * ROWS),),
        in_specs=[pl.BlockSpec(memory_space=pl.ANY)] * len(begun)
        + [block] * len(pieces)
        + [
            pl.BlockSpec(order.shape, lambda i: (0, 0)),
            pl.BlockSpec((2 * ROWS, full, full), lambda i: (i, 0, 0)),
        ],
        out_specs=pl.BlockSpec(
            (comps, parts, quads * QUAD, 2 * ROWS, full), lambda i: (0, 0, part, i, 0)
        ),
        out_shape=jax.ShapeDtypeStruct((comps, parts, slots, own, full), jnp.float32),
        scratch_shapes=[scratch, scratch],
        input_output_aliases={0: 0} if begun else {},
        compiler_params=pltpu.CompilerParams(vmem_limit_bytes=56 << 20),
        cost_estimate=pl.CostEstimate(
            flops=2 * len(pieces) * pieces[0].size * order.shape[0],
            bytes_accessed=6 * len(pieces) * pieces[0].size,
            transcendentals=0,
        ),
    )(*begun, *pieces, order, operators)


def share_degrees(sides, groups):
    me = lax.axis_index("row")
    pieces = []
    for step in range(groups):
        block = lax.dynamic_index_in_dim(sides, (me + step) % groups, keepdims=False)
        if step:
            places = [(i, (i + step) % groups) for i in range(groups)]
            block = lax.ppermute(block, "row", places)
        pieces.append(block)
    return pieces


def fits(velocity, legendre_bf, owners, groups):
    comps, parts, slots, radii, degrees = velocity.shape
    return (
        groups * radii == LANES
        and LANES % (2 * owners) == 0
        and owners % 8 == 0
        and QUAD * comps * parts * 2 * owners % LANES == 0
        and degrees % (groups * 2 * ROWS) == 0
        and velocity.shape[3] == 4 * owners
        and velocity.shape[3] % (2 * ROWS) == 0
        and velocity.shape[2] % ROWS == 0
        and (2 * legendre_bf.shape[2]) % (3 * LANES) == 0
    )


def by_radius(velocity, vorticity, order_table, legendre_bf, weighted, inverse_operators):
    owners = lax.axis_size("ma")
    slots = velocity.shape[2]
    own_orders = lax.dynamic_slice_in_dim(order_table, lax.axis_index("ma") * slots, slots)
    scale = jnp.where(own_orders == 0, 1.0, 2.0).astype(jnp.float32) / NL

    def exchange(x):
        return lax.all_to_all(x, "ma", split_axis=0, concat_axis=0, tiled=True)

    legendre = jnp.transpose(legendre_bf, (0, 2, 1))
    weights = jnp.transpose(weighted, (0, 2, 1))
    move_early, move_late = synthesize(velocity, legendre, scale)
    spin_early, spin_late = synthesize(vorticity, legendre, scale)
    move_early, spin_early = exchange(move_early), exchange(spin_early)
    move_late, spin_late = exchange(move_late), exchange(spin_late)
    table = longitude_table(order_table).reshape(2, owners, slots, NLON)
    along = jnp.transpose(table, (1, 0, 2, 3)).reshape(2 * owners * slots, NLON)
    across = jnp.transpose(along)
    early = exchange(through_grid(move_early, spin_early, across, along, NL / NLON))
    late = exchange(through_grid(move_late, spin_late, across, along, NL / NLON))
    groups = lax.axis_size("row")
    halves = [
        analyze(h, back, weights, velocity, groups) for h, back in enumerate((early, late))
    ]
    quads = ROWS // QUAD
    thirds = [
        [
            piece
            for sides in halves
            for piece in share_degrees(sides[:, i : i + quads], groups)
        ]
        for i in range(0, slots // QUAD, quads)
    ]
    order = radial_order(groups, owners, groups * velocity.shape[3], lax.axis_index("row"))
    operators = jnp.transpose(inverse_operators, (0, 2, 1)).astype(jnp.bfloat16)
    done = None
    for part, pieces in enumerate(thirds):
        done = radial_solve(pieces, order, operators, *velocity.shape[:3], part, done)
    return done


def per_device(velocity, vorticity, order_table, legendre_bf, weighted, inverse_operators):
    if fits(velocity, legendre_bf, lax.axis_size("ma"), lax.axis_size("row")):
        return by_radius(
            velocity, vorticity, order_table, legendre_bf, weighted, inverse_operators
        )
    slot_count = velocity.shape[2]
    radius_count = velocity.shape[3]
    degree_count = inverse_operators.shape[0]
    own_orders = lax.dynamic_slice_in_dim(
        order_table, lax.axis_index("ma") * slot_count, slot_count
    )
    own_scale = jnp.where(own_orders == 0, 1.0, 2.0).astype(jnp.float32) / NL
    harmonics = longitude_table(order_table)

    def arrange(grid_values):
        scaled = (grid_values * own_scale[None, None, :, None, None]).astype(jnp.bfloat16)
        ordered = jnp.transpose(scaled, (0, 1, 2, 4, 3))
        return ordered.reshape(3, 2, slot_count, NLAT * radius_count)

    def synthesize(spectral):
        grid_values = jnp.einsum(
            "cpsrl,slt->cpsrt", spectral, legendre_bf, preferred_element_type=jnp.float32
        )
        return arrange(grid_values)

    def to_longitude(pieces):
        return jnp.einsum("cpsk,psn->ckn", pieces, harmonics, preferred_element_type=jnp.float32)

    velocity_grid = to_longitude(
        lax.all_to_all(synthesize(velocity), "ma", split_axis=3, concat_axis=2, tiled=True)
    )
    vorticity_grid = to_longitude(
        lax.all_to_all(synthesize(vorticity), "ma", split_axis=3, concat_axis=2, tiled=True)
    )
    products = jnp.stack(cross_terms(velocity_grid, vorticity_grid)).astype(jnp.bfloat16)
    spectral_back = jnp.einsum(
        "ckn,psn->cpsk", products, harmonics, preferred_element_type=jnp.float32
    )
    spectral_back = (NL / NLON * spectral_back).astype(jnp.bfloat16)
    pieces = lax.all_to_all(spectral_back, "ma", split_axis=2, concat_axis=3, tiled=True)
    field_count = pieces.shape[0]
    split_pieces = pieces.reshape(field_count, 2, slot_count, NLAT, radius_count)
    terms = jnp.einsum(
        "cpstr,slt->cpslr", split_pieces, weighted, preferred_element_type=jnp.float32
    )
    spec_terms = terms.reshape(field_count, 2, slot_count, NL * radius_count)
    velocity_terms = jnp.transpose(velocity.astype(jnp.float32), (0, 1, 2, 4, 3)).reshape(
        3, 2, slot_count, NL * radius_count
    )
    right_side = velocity_terms + time_step * spec_terms
    right_side = right_side.reshape(3, 2, slot_count, 1, NL * radius_count)
    operator_blocks = inverse_operators.reshape(degree_count, NR, NR // radius_count, radius_count)
    pieces = lax.all_to_all(
        right_side.astype(jnp.bfloat16), "row", split_axis=4, concat_axis=3, tiled=True
    ).astype(right_side.dtype)
    field_count = pieces.shape[0]
    columns = pieces.reshape(
        field_count, 2, slot_count, NR // radius_count, degree_count, radius_count
    )
    return jnp.einsum(
        "cpsqlr,laqr->cpsla", columns, operator_blocks, precision=lax.Precision.HIGHEST
    )


def solution(mesh):
    in_specs = (
        P(None, None, "ma", "row", None),
        P(None, None, "ma", "row", None),
        P(),
        P("ma", None, None),
        P("ma", None, None),
        P("row", None, None),
    )
    out_specs = P(None, None, "ma", "row", None)
    return jax.shard_map(
        per_device, mesh=mesh, in_specs=in_specs, out_specs=out_specs, check_vma=False
    )
```
